32 devices in a mesh: groups: 2 (over y), dp: 4 (over x, core), tensor: 4 (over z).
Axes of the slice: x: 2, y: 2, z: 4, core: 2. Of those that a mesh axis runs over, the one named last changes fastest.
Arguments:
- tokens: bfloat16 [6144, 5120], P(('groups', 'dp'), 'tensor'), parts along dimension 0, may hold values from -6 to 6
- lengths: int32 [8, 2], P(('groups', 'dp')), parts along dimension 0, may hold values from 192 to 576, as said below
- owner_slot: int32 [16], P('groups'), parts along dimension 0, may hold values from 0 to 7, each once
- norm_gain: bfloat16 [5120], replicated, may hold values from 0.5 to 1.5
- w_query: bfloat16 [5120, 4096], P('dp', 'tensor'), may hold values from -0.078125 to 0.078125
- w_key: bfloat16 [5120, 1024], P('dp', 'tensor'), may hold values from -0.078125 to 0.078125
- w_value: bfloat16 [5120, 1024], P('dp', 'tensor'), may hold values from -0.078125 to 0.078125
- q_gain: bfloat16 [128], replicated, may hold values from 0.5 to 8
- k_gain: bfloat16 [128], replicated, may hold values from 0.5 to 8
- w_out: bfloat16 [4096, 5120], P('tensor', 'dp'), may hold values from -0.09375 to 0.09375
Outputs:
- mixed: bfloat16 [6144, 5120], P(('groups', 'dp'), 'tensor'), parts along dimension 0
- k_cache: bfloat16 [16, 576, 1024], P(('groups', 'dp'), None, 'tensor'), parts along dimension 0
- v_cache: bfloat16 [16, 576, 1024], P(('groups', 'dp'), None, 'tensor'), parts along dimension 0
The draws below stay inside these ranges and needn't reach their ends.
There are 2 independent parts, one for each index of `groups`. The reference program is written for one: setup_inputs(seed, part) draws one part's arguments, and reference() takes and returns one part's arrays. A program takes and returns all parts, laid end to end along the dimension named above; an argument that names none is the same for every part. Nothing has to cross between parts.
Inputs may be any that keep to these rules, and one draw needn't show every extreme that they name: `lengths`: each replica's prompts sum to 768 rows; in every draw some prompt has exactly 576 rows. `owner_slot`: a permutation of the slots.
All inputs are finite; a program needn't handle non-finite values.
Results may differ from the reference program's by a relative error of at most 0.01.
The reference program's roundings to bfloat16 on the way count: a program that leaves them out, or rounds other values in their place, can miss the bound.
Values may be sent and summed in bfloat16 or wider, within the bound.
A program may use at most 128 MiB of HBM per device.

```python
import jax
import jax.numpy as jnp
from jax import lax

D = 5120
HQ = 32
KEY_VALUE_HEADS = 8
HEAD_SIZE = 128
REPLICA_TOKENS = 768
MOST = 576
TOKENS = 3072
SLOTS = 8
N_DP = 4
N_TENSOR = 4


def draw_lengths(key, part):
    key = jax.random.fold_in(key, 11)
    first_key, pick_key, flip_key = jax.random.split(key, 3)
    first = jax.random.randint(first_key, (N_DP,), REPLICA_TOKENS - MOST, MOST + 1, dtype=jnp.int32)
    chosen = jax.random.randint(pick_key, (), 0, N_DP, dtype=jnp.int32)
    first = jnp.where(jnp.arange(N_DP, dtype=jnp.int32) == chosen, MOST, first).astype(jnp.int32)
    flips = jax.random.randint(flip_key, (N_DP,), 0, 2, dtype=jnp.int32)
    leading = jnp.where(flips == 1, REPLICA_TOKENS - first, first).astype(jnp.int32)
    return jnp.stack([leading, REPLICA_TOKENS - leading], axis=1).astype(jnp.int32)


def draw_q_gain(key, part):
    key = jax.random.fold_in(key, 21)
    values = jax.random.uniform(key, (HEAD_SIZE,), jnp.float32, 0.5, 2.5)
    return values.astype(jnp.bfloat16)


def draw_k_gain(key, part):
    key = jax.random.fold_in(key, 37)
    values = jax.random.uniform(key, (HEAD_SIZE,), jnp.float32, 0.5, 2.5)
    return values.astype(jnp.bfloat16)


def steps_of(key, dims, cuts, smallest, largest):
    level, own = 1.0, jax.random.fold_in(key, 6)
    for dim, shards_of in cuts:
        steps = jnp.exp(jax.random.uniform(jax.random.fold_in(own, dim), (shards_of,), jnp.float32, smallest / len(cuts), largest / len(cuts)))
        level = level * jnp.repeat(steps, dims[dim] // shards_of).reshape([-1 if axis == dim else 1 for axis in range(len(dims))])
    return level


def noise(key, extent, spread, reach, shards=(), kind=jnp.bfloat16):
    entries = spread * jax.random.normal(key, extent, jnp.float32)
    if shards:
        entries = entries * steps_of(key, extent, shards, -0.22, 0.18)
    return jnp.clip(entries, -reach, reach).astype(kind)


def setup_inputs(seed: int = 0, part: int = 0) -> dict:
    streams_of = jax.random.split(jax.random.key(seed), 11)
    own_keys = jax.random.split(jax.random.fold_in(streams_of[10], part), 11)
    tokens = noise(own_keys[0], (TOKENS, D), 1.0, 6.0, ((0, 4), (1, 4)))
    lengths = draw_lengths(jax.random.fold_in(jax.random.fold_in(streams_of[10], part), 71), part)
    owner_slot = jax.random.permutation(own_keys[2], SLOTS).astype(jnp.int32)
    norm_gain = jnp.clip(1.0 + 0.1 * jax.random.normal(streams_of[3], (D,), jnp.float32), 0.5, 1.5).astype(jnp.bfloat16)
    w_query = noise(streams_of[4], (D, HQ * HEAD_SIZE), D ** -0.5, 0.078125, ((0, 4), (1, 4)))
    w_key = noise(streams_of[5], (D, KEY_VALUE_HEADS * HEAD_SIZE), D ** -0.5, 0.078125, ((0, 4), (1, 4)))
    w_value = noise(streams_of[6], (D, KEY_VALUE_HEADS * HEAD_SIZE), D ** -0.5, 0.078125, ((0, 4), (1, 4)))
    q_gain = draw_q_gain(jax.random.fold_in(streams_of[10], 71), part)
    k_gain = draw_k_gain(jax.random.fold_in(streams_of[10], 71), part)
    w_out = noise(streams_of[9], (HQ * HEAD_SIZE, D), (HQ * HEAD_SIZE) ** -0.5, 0.09375, ((0, 4), (1, 4)))
    return dict(tokens=tokens, lengths=lengths, owner_slot=owner_slot, norm_gain=norm_gain, w_query=w_query, w_key=w_key, w_value=w_value, q_gain=q_gain, k_gain=k_gain, w_out=w_out)


EPS = 1e-06
THETA = 1000000.0

def head_norm(t, gain):
    return t * lax.rsqrt(lax.optimization_barrier(jnp.mean(t * t, axis=-1, keepdims=True)) + EPS) * gain.astype(jnp.float32)

def rotate(t, positions):
    half = t.shape[-1] // 2
    freq = THETA ** (-(2.0 * jnp.arange(half, dtype=jnp.float32)) / t.shape[-1])
    angle = positions.astype(jnp.float32)[:, None] * freq[None, :]
    cosine = jnp.cos(angle)[:, None, :]
    sine = jnp.sin(angle)[:, None, :]
    first, second = (t[..., :half], t[..., half:])
    return jnp.concatenate([first * cosine - second * sine, second * cosine + first * sine], axis=-1)

def layout(lens, token_rows):
    local = jnp.arange(token_rows, dtype=jnp.int32)
    ends = jnp.cumsum(lens).astype(jnp.int32)
    starts = (ends - lens).astype(jnp.int32)
    segment_ids = lax.optimization_barrier(jnp.sum((local[:, None] >= ends[None, :]).astype(jnp.int32), axis=1)).astype(jnp.int32)
    chosen = segment_ids[:, None] == jnp.arange(lens.shape[0], dtype=jnp.int32)[None, :]
    begin = lax.optimization_barrier(jnp.sum(jnp.where(chosen, starts[None, :], 0), axis=1)).astype(jnp.int32)
    return (segment_ids, (local - begin).astype(jnp.int32), starts)

def attend_baseline(query_rotated, key_rotated, value_rotated, segment_ids, positions):
    token_rows, heads, size = query_rotated.shape
    key_value_count = key_rotated.shape[1]
    grouped = query_rotated.astype(jnp.float32).reshape(token_rows, key_value_count, heads // key_value_count, size)
    scores = jnp.einsum('qngd,knd->ngqk', grouped, key_rotated.astype(jnp.float32)) / jnp.sqrt(jnp.float32(size))
    allowed = (segment_ids[:, None] == segment_ids[None, :]) & (positions[None, :] <= positions[:, None])
    scores = jnp.where(allowed[None, None], scores, -1e+30)
    top = lax.optimization_barrier(jnp.max(scores, axis=-1, keepdims=True))
    expo = jnp.exp(scores - top)
    weight_params = (expo / lax.optimization_barrier(jnp.sum(expo, axis=-1, keepdims=True))).astype(jnp.bfloat16)
    block_output = jnp.einsum('suof,fsc->osuc', weight_params.astype(jnp.float32), value_rotated.astype(jnp.float32))
    return block_output.reshape(token_rows, heads * size).astype(jnp.bfloat16)

def pack(key_value_pair, lens, starts, longest):
    padded = jnp.concatenate([key_value_pair, jnp.zeros((longest, key_value_pair.shape[1]), key_value_pair.dtype)], axis=0)
    blocks = []
    for prompt in range(lens.shape[0]):
        block = lax.dynamic_slice_in_dim(padded, starts[prompt], longest, 0)
        live = jnp.arange(longest, dtype=jnp.int32)[:, None] < lens[prompt]
        blocks.append(jnp.where(live, block, jnp.zeros_like(block)))
    return jnp.stack(blocks, axis=0)

def reference(tokens, lengths, owner_slot, norm_gain, w_query, w_key, w_value, q_gain, k_gain, w_out):
    wide = tokens.astype(jnp.float32)
    normed = (wide * lax.rsqrt(lax.optimization_barrier(jnp.mean(wide * wide, axis=-1, keepdims=True)) + EPS) * norm_gain.astype(jnp.float32)).astype(jnp.bfloat16)
    query = jnp.dot(normed, w_query, preferred_element_type=jnp.float32)
    key = jnp.dot(normed, w_key, preferred_element_type=jnp.float32)
    value_matrix = jnp.dot(normed, w_value, preferred_element_type=jnp.float32)

    def replica(inputs):
        q_rows, k_rows, value_rows, lens = inputs
        segment_ids, positions, starts = layout(lens, REPLICA_TOKENS)
        query_rotated = rotate(head_norm(q_rows.reshape(REPLICA_TOKENS, HQ, HEAD_SIZE), q_gain), positions).astype(jnp.bfloat16)
        key_rotated = rotate(head_norm(k_rows.reshape(REPLICA_TOKENS, KEY_VALUE_HEADS, HEAD_SIZE), k_gain), positions).astype(jnp.bfloat16)
        value_rotated = value_rows.reshape(REPLICA_TOKENS, KEY_VALUE_HEADS, HEAD_SIZE).astype(jnp.bfloat16)
        attended_rows = attend_baseline(query_rotated, key_rotated, value_rotated, segment_ids, positions)
        key_value_pair = jnp.concatenate([key_rotated.reshape(REPLICA_TOKENS, KEY_VALUE_HEADS * HEAD_SIZE), value_rotated.reshape(REPLICA_TOKENS, KEY_VALUE_HEADS * HEAD_SIZE)], axis=1)
        return (attended_rows, pack(key_value_pair, lens, starts, MOST))
    attended_rows, compact = lax.map(replica, (query.reshape(N_DP, REPLICA_TOKENS, HQ * HEAD_SIZE), key.reshape(N_DP, REPLICA_TOKENS, KEY_VALUE_HEADS * HEAD_SIZE), value_matrix.reshape(N_DP, REPLICA_TOKENS, KEY_VALUE_HEADS * HEAD_SIZE), lengths))
    attended_rows = attended_rows.reshape(TOKENS, HQ * HEAD_SIZE)
    share = HQ * HEAD_SIZE // N_TENSOR
    summed = jnp.zeros((TOKENS, D), jnp.float32)
    for group in range(N_TENSOR):
        partial_value = jnp.dot(attended_rows[:, group * share:(group + 1) * share], w_out[group * share:(group + 1) * share], preferred_element_type=jnp.float32)
        summed = summed + partial_value.astype(jnp.bfloat16).astype(jnp.float32)
    mixed = (wide + summed).astype(jnp.bfloat16)
    compact = compact.reshape(SLOTS, MOST, 2 * KEY_VALUE_HEADS * HEAD_SIZE)
    cache = jnp.zeros_like(compact).at[owner_slot].set(compact)
    return (mixed, cache[..., :KEY_VALUE_HEADS * HEAD_SIZE], cache[..., KEY_VALUE_HEADS * HEAD_SIZE:])
```

```python
import functools

import jax
import jax.numpy as jnp
from jax import lax
from jax.sharding import PartitionSpec as P

HEAD_SIZE = 128
PROMPTS = 2
MOST = 576
HALVES = 2


EPS = 1e-06
THETA = 1000000.0


def head_norm(t, gain):
    return t * lax.rsqrt(jnp.mean(t * t, axis=-1, keepdims=True) + EPS) * gain.astype(jnp.float32)


def rotate(t, positions):
    half = t.shape[-1] // 2
    freq = THETA ** (-(2.0 * jnp.arange(half, dtype=jnp.float32)) / t.shape[-1])
    angle = positions.astype(jnp.float32)[:, None] * freq[None, :]
    cosine = jnp.cos(angle)[:, None, :]
    sine = jnp.sin(angle)[:, None, :]
    first, second = (t[..., :half], t[..., half:])
    return jnp.concatenate(
        [first * cosine - second * sine, second * cosine + first * sine], axis=-1
    )


def layout(lens, token_rows):
    local = jnp.arange(token_rows, dtype=jnp.int32)
    ends = jnp.cumsum(lens)
    starts = ends - lens
    segment_ids = jnp.sum((local[:, None] >= ends[None, :]).astype(jnp.int32), axis=1)
    chosen = segment_ids[:, None] == jnp.arange(lens.shape[0], dtype=jnp.int32)[None, :]
    begin = jnp.sum(jnp.where(chosen, starts[None, :], 0), axis=1)
    return (segment_ids, local - begin, starts)


def attend_heads(query_rotated, key_rotated, value_rotated, segment_ids, first_row):
    token_rows, heads, size = query_rotated.shape
    key_rows, key_value_count = key_rotated.shape[:2]
    grouped = query_rotated.reshape(token_rows, key_value_count, heads // key_value_count, size)
    scores = jnp.einsum(
        "qngd,knd->ngqk", grouped, key_rotated, preferred_element_type=jnp.float32
    ) / jnp.sqrt(jnp.float32(size))
    query_row = first_row + jnp.arange(token_rows, dtype=jnp.int32)
    key_row = jnp.arange(key_rows, dtype=jnp.int32)
    own = segment_ids[first_row : first_row + token_rows]
    allowed = (own[:, None] == segment_ids[None, :key_rows]) & (
        key_row[None, :] <= query_row[:, None]
    )
    scores = jnp.where(allowed[None, None], scores, -1e30)
    top = jnp.max(scores, axis=-1, keepdims=True)
    expo = jnp.exp(scores - top)
    weight_params = (expo / jnp.sum(expo, axis=-1, keepdims=True)).astype(jnp.bfloat16)
    block_output = jnp.einsum(
        "suof,fsc->osuc", weight_params, value_rotated, preferred_element_type=jnp.float32
    )
    return block_output.reshape(token_rows, heads * size).astype(jnp.bfloat16)


def swap(block, axis, pairs):
    return lax.ppermute(block, axis, pairs)


def gather_blocks(shard, n_groups, n_dp, cuts):
    chips = n_dp // 2
    twin = [(i, i ^ 1) for i in range(n_dp)]
    onward = [(i, (i + 2) % n_dp) for i in range(n_dp)]
    me = lax.axis_index("dp")
    group = lax.axis_index("groups")
    rows = shard.shape[0]
    blocks = [(me, 0, shard), (me ^ 1, 0, swap(shard, "dp", twin))]
    part = rows // (n_groups * cuts)
    for cut in range(cuts):
        base = cut * n_groups * part
        piece = lax.dynamic_slice_in_dim(shard, base + group * part, part, 0)
        for step in range(1, chips):
            piece = swap(piece, "dp", onward)
            owner = lax.rem(me - 2 * step + n_dp, n_dp)
            got = [(owner, base + group * part, piece)]
            for turn in range(1, n_groups):
                other = swap(piece, "groups", [(i, (i + turn) % n_groups) for i in range(n_groups)])
                source = lax.rem(group - turn + n_groups, n_groups)
                got.append((owner, base + source * part, other))
            for owner_, row, block in got:
                blocks.append((owner_, row, block))
            for owner_, row, block in got:
                blocks.append((owner_ ^ 1, row, swap(block, "dp", twin)))
    return blocks


def gather_rows(rows_block, n_dp):
    chips = n_dp // 2
    twin = [(i, i ^ 1) for i in range(n_dp)]
    onward = [(i, (i + 2) % n_dp) for i in range(n_dp)]
    me = lax.axis_index("dp")
    blocks = []
    piece = rows_block
    for step in range(chips):
        if step:
            piece = swap(piece, "dp", onward)
        owner = lax.rem(me - 2 * step + n_dp, n_dp)
        blocks.append((owner, piece))
        blocks.append((owner ^ 1, swap(piece, "dp", twin)))
    return blocks


def on_device(
    n_groups, n_dp, tokens, lengths, owner_slot, norm_gain, w_query, w_key, w_value, q_gain, k_gain, w_out
):
    token_rows = tokens.shape[0]
    half = token_rows // HALVES
    q_width, kv_width = w_query.shape[1], w_key.shape[1]
    q_heads, key_value_count = q_width // HEAD_SIZE, kv_width // HEAD_SIZE
    depth = w_query.shape[0]
    wholes = [
        lax.all_gather(tokens[h * half : (h + 1) * half], "tensor", axis=1, tiled=True)
        for h in range(HALVES)
    ]
    w_all = jnp.concatenate([w_key, w_value, w_query], axis=1)
    in_blocks = gather_blocks(w_all, n_groups, n_dp, 2)
    out_blocks = gather_blocks(w_out, n_groups, n_dp, 1)
    lens = lengths[0]
    segment_ids, positions, starts = layout(lens, token_rows)

    out_full = jnp.zeros((w_out.shape[0], w_out.shape[1] * n_dp), w_out.dtype)
    for owner, row, block in out_blocks:
        out_full = lax.dynamic_update_slice(out_full, block, (row, owner * w_out.shape[1]))

    keys, values, mixed = [], [], []
    for h in range(HALVES):
        wide = wholes[h].astype(jnp.float32)
        normed = (
            wide
            * lax.rsqrt(jnp.mean(wide * wide, axis=-1, keepdims=True) + EPS)
            * norm_gain.astype(jnp.float32)
        ).astype(jnp.bfloat16)
        total = None
        for owner, row, block in in_blocks:
            columns = lax.dynamic_slice_in_dim(normed, owner * depth + row, block.shape[0], 1)
            term = jnp.dot(columns, block, preferred_element_type=jnp.float32)
            total = term if total is None else total + term
        key, value_matrix, query = (
            total[:, :kv_width],
            total[:, kv_width : 2 * kv_width],
            total[:, 2 * kv_width :],
        )
        here = slice(h * half, (h + 1) * half)
        query_rotated = rotate(
            head_norm(query.reshape(half, q_heads, HEAD_SIZE), q_gain), positions[here]
        ).astype(jnp.bfloat16)
        keys.append(
            rotate(
                head_norm(key.reshape(half, key_value_count, HEAD_SIZE), k_gain), positions[here]
            ).astype(jnp.bfloat16)
        )
        values.append(
            value_matrix.reshape(half, key_value_count, HEAD_SIZE).astype(jnp.bfloat16)
        )
        attended_rows = attend_heads(
            query_rotated,
            jnp.concatenate(keys, axis=0),
            jnp.concatenate(values, axis=0),
            segment_ids,
            h * half,
        )
        term = jnp.dot(attended_rows, out_full, preferred_element_type=jnp.float32)
        summed = lax.psum_scatter(
            term.astype(jnp.bfloat16), "tensor", scatter_dimension=1, tiled=True
        ).astype(jnp.float32)
        mixed.append((tokens[here].astype(jnp.float32) + summed).astype(jnp.bfloat16))

    pair = jnp.concatenate(
        [
            jnp.concatenate(keys, axis=0).reshape(token_rows, kv_width),
            jnp.concatenate(values, axis=0).reshape(token_rows, kv_width),
        ],
        axis=1,
    )
    stack = jnp.zeros((n_dp * token_rows + MOST, 2 * kv_width), jnp.bfloat16)
    for owner, block in gather_rows(pair, n_dp):
        stack = lax.dynamic_update_slice(stack, block, (owner * token_rows, 0))
    every_length = jnp.zeros((n_dp, PROMPTS), jnp.int32)
    for owner, block in gather_rows(lengths, n_dp):
        every_length = lax.dynamic_update_slice(every_length, block, (owner, 0))
    replica = lax.axis_index("dp")
    slots = []
    for p in range(PROMPTS):
        prompt = jnp.argmax(owner_slot == replica * PROMPTS + p).astype(jnp.int32)
        length = every_length[prompt // PROMPTS, prompt % PROMPTS]
        before = jnp.where(
            jnp.arange(PROMPTS) < prompt % PROMPTS, every_length[prompt // PROMPTS], 0
        ).sum()
        block = lax.dynamic_slice_in_dim(
            stack, prompt // PROMPTS * token_rows + before, MOST, 0
        )
        live = jnp.arange(MOST, dtype=jnp.int32)[:, None] < length
        slots.append(jnp.where(live, block, jnp.zeros_like(block)))
    cache = jnp.stack(slots, axis=0)
    return (jnp.concatenate(mixed, axis=0), cache[..., :kv_width], cache[..., kv_width:])


def solution(mesh):
    return jax.shard_map(
        functools.partial(on_device, mesh.shape["groups"], mesh.shape["dp"]),
        mesh=mesh,
        in_specs=(
            P(("groups", "dp"), "tensor"),
            P(("groups", "dp"), None),
            P("groups"),
            P(),
            P("dp", "tensor"),
            P("dp", "tensor"),
            P("dp", "tensor"),
            P(),
            P(),
            P("tensor", "dp"),
        ),
        out_specs=(
            P(("groups", "dp"), "tensor"),
            P(("groups", "dp"), None, "tensor"),
            P(("groups", "dp"), None, "tensor"),
        ),
        check_vma=False,
    )
```

```python
import functools

import jax
import jax.numpy as jnp
from jax import lax
from jax.experimental import pallas as pl
from jax.experimental.pallas import tpu as pltpu
from jax.sharding import PartitionSpec as P

HEAD_SIZE = 128
PROMPTS = 2
MOST = 576
CHUNKS = 3


EPS = 1e-06
THETA = 1000000.0


def layout(lens, token_rows):
    local = jnp.arange(token_rows, dtype=jnp.int32)
    ends = jnp.cumsum(lens)
    starts = ends - lens
    segment_ids = jnp.sum((local[:, None] >= ends[None, :]).astype(jnp.int32), axis=1)
    chosen = segment_ids[:, None] == jnp.arange(lens.shape[0], dtype=jnp.int32)[None, :]
    begin = jnp.sum(jnp.where(chosen, starts[None, :], 0), axis=1)
    return (segment_ids, local - begin, starts)


def turn_heads(t, gain, cosine, sine):
    t = t * lax.rsqrt(jnp.mean(t * t, axis=-1, keepdims=True) + EPS) * gain
    return (t * cosine + pltpu.roll(t, HEAD_SIZE // 2, 1) * sine).astype(jnp.bfloat16)


def attend_kernel(chunk, kv_heads, q_heads, *refs):
    total, cosine, sine, begin, q_gain, k_gain = refs[:6]
    past_keys, past_values = refs[6 : 6 + chunk], refs[6 + chunk : 6 + 2 * chunk]
    attended, key_out, value_out = refs[6 + 2 * chunk :]
    rows = total.shape[0]
    group = q_heads // kv_heads
    kv_width = kv_heads * HEAD_SIZE
    cos, sin = cosine[...], sine[...]
    q_scale, k_scale = q_gain[...].astype(jnp.float32), k_gain[...].astype(jnp.float32)
    keys = (chunk + 1) * rows
    key_row = lax.broadcasted_iota(jnp.int32, (rows, keys), 1)
    query_row = lax.broadcasted_iota(jnp.int32, (rows, keys), 0) + chunk * rows
    allowed = (key_row <= query_row) & (key_row >= begin[...])
    value_out[...] = total[:, kv_width : 2 * kv_width].astype(jnp.bfloat16)
    for n in range(kv_heads):
        here = slice(n * HEAD_SIZE, (n + 1) * HEAD_SIZE)
        key_out[:, here] = turn_heads(total[:, here], k_scale, cos, sin)
        key = jnp.concatenate([k[:, here] for k in past_keys] + [key_out[:, here]], axis=0)
        value = jnp.concatenate([v[:, here] for v in past_values] + [value_out[:, here]], axis=0)
        for g in range(group):
            first = (n * group + g) * HEAD_SIZE
            query = turn_heads(
                total[:, 2 * kv_width + first : 2 * kv_width + first + HEAD_SIZE], q_scale, cos, sin
            )
            scores = lax.dot_general(
                query, key, (((1,), (1,)), ((), ())), preferred_element_type=jnp.float32
            ) / (HEAD_SIZE**0.5)
            scores = jnp.where(allowed, scores, -1e30)
            expo = jnp.exp(scores - jnp.max(scores, axis=-1, keepdims=True))
            weights = (expo / jnp.sum(expo, axis=-1, keepdims=True)).astype(jnp.bfloat16)
            attended[:, first : first + HEAD_SIZE] = jnp.dot(
                weights, value, preferred_element_type=jnp.float32
            ).astype(jnp.bfloat16)


def attend_chunk(chunk, total, cosine, sine, begin, q_gain, k_gain, keys, values, kv_width):
    rows = total.shape[0]
    q_width = total.shape[1] - 2 * kv_width
    flops = 4 * rows * (chunk + 1) * rows * q_width
    return pl.pallas_call(
        functools.partial(attend_kernel, chunk, kv_width // HEAD_SIZE, q_width // HEAD_SIZE),
        out_shape=(
            jax.ShapeDtypeStruct((rows, q_width), jnp.bfloat16),
            jax.ShapeDtypeStruct((rows, kv_width), jnp.bfloat16),
            jax.ShapeDtypeStruct((rows, kv_width), jnp.bfloat16),
        ),
        compiler_params=pltpu.CompilerParams(vmem_limit_bytes=32 * 2**20),
        cost_estimate=pl.CostEstimate(
            flops=4 * flops, bytes_accessed=4 * total.size, transcendentals=0
        ),
    )(total, cosine, sine, begin, q_gain, k_gain, *keys, *values)


def swap(block, axis, pairs):
    return lax.ppermute(block, axis, pairs)


def gather_blocks(shard, n_groups, n_dp, cuts):
    chips = n_dp // 2
    twin = [(i, i ^ 1) for i in range(n_dp)]
    onward = [(i, (i + 2) % n_dp) for i in range(n_dp)]
    me = lax.axis_index("dp")
    group = lax.axis_index("groups")
    rows = shard.shape[0]
    blocks = [(me, 0, shard), (me ^ 1, 0, swap(shard, "dp", twin))]
    part = rows // (n_groups * cuts)
    for cut in range(cuts):
        base = cut * n_groups * part
        piece = lax.dynamic_slice_in_dim(shard, base + group * part, part, 0)
        for step in range(1, chips):
            piece = swap(piece, "dp", onward)
            owner = lax.rem(me - 2 * step + n_dp, n_dp)
            got = [(owner, base + group * part, piece)]
            for turn in range(1, n_groups):
                other = swap(piece, "groups", [(i, (i + turn) % n_groups) for i in range(n_groups)])
                source = lax.rem(group - turn + n_groups, n_groups)
                got.append((owner, base + source * part, other))
            for owner_, row, block in got:
                blocks.append((owner_, row, block))
            for owner_, row, block in got:
                blocks.append((owner_ ^ 1, row, swap(block, "dp", twin)))
    return blocks


def whole_rows(blocks, n_dp, depth):
    full = jnp.zeros((n_dp * depth, blocks[0][2].shape[1]), blocks[0][2].dtype)
    for owner, row, block in blocks:
        full = lax.dynamic_update_slice(full, block, (owner * depth + row, 0))
    return full


def gather_rows(rows_block, n_dp):
    chips = n_dp // 2
    twin = [(i, i ^ 1) for i in range(n_dp)]
    onward = [(i, (i + 2) % n_dp) for i in range(n_dp)]
    me = lax.axis_index("dp")
    blocks = []
    piece = rows_block
    for step in range(chips):
        if step:
            piece = swap(piece, "dp", onward)
        owner = lax.rem(me - 2 * step + n_dp, n_dp)
        blocks.append((owner, piece))
        blocks.append((owner ^ 1, swap(piece, "dp", twin)))
    return blocks


def on_device(
    n_groups, n_dp, n_tensor, tokens, lengths, owner_slot, norm_gain, w_query, w_key, w_value, q_gain, k_gain, w_out
):
    token_rows = tokens.shape[0]
    rows_each = token_rows // CHUNKS
    kv_width = w_key.shape[1]
    depth = w_query.shape[0]
    wholes = [
        lax.all_gather(tokens[h * rows_each : (h + 1) * rows_each], "tensor", axis=1, tiled=True)
        for h in range(CHUNKS)
    ]
    w_all = jnp.concatenate([w_key, w_value, w_query], axis=1)
    in_full = whole_rows(gather_blocks(w_all, n_groups, n_dp, 2), n_dp, depth)
    out_blocks = gather_blocks(w_out, n_groups, n_dp, 1)
    lens = lengths[0]
    segment_ids, positions, starts = layout(lens, token_rows)
    begin = (jnp.arange(token_rows, dtype=jnp.int32) - positions)[:, None]
    freq = THETA ** (-(2.0 * jnp.arange(HEAD_SIZE // 2, dtype=jnp.float32)) / HEAD_SIZE)
    angle = positions.astype(jnp.float32)[:, None] * freq[None, :]
    cosine, sine = jnp.cos(angle), jnp.sin(angle)
    cosine = jnp.concatenate([cosine, cosine], axis=1)
    sine = jnp.concatenate([-sine, sine], axis=1)

    order = []
    for owner, row, block in out_blocks:
        if block.shape[0] == w_out.shape[0]:
            order.append((owner, block))
    rest = [b for b in out_blocks if b[2].shape[0] != w_out.shape[0]]
    for first in range(0, len(rest), 2 * n_groups):
        for lane in range(2):
            parts = rest[first + lane * n_groups : first + (lane + 1) * n_groups]
            whole = jnp.zeros_like(w_out)
            for owner, row, block in parts:
                whole = lax.dynamic_update_slice(whole, block, (row, 0))
            order.append((parts[0][0], whole))

    keys, values, mixed = [], [], []
    last = None
    for h in range(CHUNKS):
        here = slice(h * rows_each, (h + 1) * rows_each)
        whole = wholes[h]
        if last is not None:
            whole, last = lax.optimization_barrier((whole, last))
        wide = whole.astype(jnp.float32)
        normed = (
            wide
            * lax.rsqrt(jnp.mean(wide * wide, axis=-1, keepdims=True) + EPS)
            * norm_gain.astype(jnp.float32)
        ).astype(jnp.bfloat16)
        total = jnp.dot(normed, in_full, preferred_element_type=jnp.float32)
        attended_rows, key, value = attend_chunk(
            h, total, cosine[here], sine[here], begin[here], q_gain[None], k_gain[None], keys, values, kv_width
        )
        keys.append(key)
        values.append(value)
        term = jnp.zeros((rows_each, w_out.shape[1] * n_dp), jnp.bfloat16)
        for owner, block in order:
            part = jnp.dot(attended_rows, block, preferred_element_type=jnp.float32)
            term = lax.dynamic_update_slice(
                term, part.astype(jnp.bfloat16), (0, owner * w_out.shape[1])
            )
        last = term
        width = tokens.shape[1]
        rank = lax.axis_index("tensor")
        summed = lax.dynamic_slice_in_dim(term, rank * width, width, 1).astype(jnp.float32)
        for turn in range(1, n_tensor):
            target = lax.rem(rank + turn, n_tensor)
            piece = lax.dynamic_slice_in_dim(term, target * width, width, 1)
            got = swap(piece, "tensor", [(i, (i + turn) % n_tensor) for i in range(n_tensor)])
            summed = summed + got.astype(jnp.float32)
        mixed.append((tokens[here].astype(jnp.float32) + summed).astype(jnp.bfloat16))

    pair = jnp.concatenate(
        [
            jnp.concatenate(keys, axis=0),
            jnp.concatenate(values, axis=0),
        ],
        axis=1,
    )
    stack = jnp.zeros((n_dp * token_rows + MOST, 2 * kv_width), jnp.bfloat16)
    for owner, block in gather_rows(pair, n_dp):
        stack = lax.dynamic_update_slice(stack, block, (owner * token_rows, 0))
    every_length = jnp.zeros((n_dp, PROMPTS), jnp.int32)
    for owner, block in gather_rows(lengths, n_dp):
        every_length = lax.dynamic_update_slice(every_length, block, (owner, 0))
    replica = lax.axis_index("dp")
    slots = []
    for p in range(PROMPTS):
        prompt = jnp.argmax(owner_slot == replica * PROMPTS + p).astype(jnp.int32)
        length = every_length[prompt // PROMPTS, prompt % PROMPTS]
        before = jnp.where(
            jnp.arange(PROMPTS) < prompt % PROMPTS, every_length[prompt // PROMPTS], 0
        ).sum()
        block = lax.dynamic_slice_in_dim(
            stack, prompt // PROMPTS * token_rows + before, MOST, 0
        )
        live = jnp.arange(MOST, dtype=jnp.int32)[:, None] < length
        slots.append(jnp.where(live, block, jnp.zeros_like(block)))
    cache = jnp.stack(slots, axis=0)
    return (jnp.concatenate(mixed, axis=0), cache[..., :kv_width], cache[..., kv_width:])


def solution(mesh):
    return jax.shard_map(
        functools.partial(on_device, mesh.shape["groups"], mesh.shape["dp"], mesh.shape["tensor"]),
        mesh=mesh,
        in_specs=(
            P(("groups", "dp"), "tensor"),
            P(("groups", "dp"), None),
            P("groups"),
            P(),
            P("dp", "tensor"),
            P("dp", "tensor"),
            P("dp", "tensor"),
            P(),
            P(),
            P("tensor", "dp"),
        ),
        out_specs=(
            P(("groups", "dp"), "tensor"),
            P(("groups", "dp"), None, "tensor"),
            P(("groups", "dp"), None, "tensor"),
        ),
        check_vma=False,
    )
```

```python
import functools

import jax
import jax.numpy as jnp
from jax import lax
from jax.experimental import pallas as pl
from jax.experimental.pallas import tpu as pltpu
from jax.sharding import PartitionSpec as P

HEAD_SIZE = 128
PROMPTS = 2
MOST = 576
CHUNKS = 3


EPS = 1e-06
THETA = 1000000.0


def layout(lens, token_rows):
    local = jnp.arange(token_rows, dtype=jnp.int32)
    ends = jnp.cumsum(lens)
    starts = ends - lens
    segment_ids = jnp.sum((local[:, None] >= ends[None, :]).astype(jnp.int32), axis=1)
    chosen = segment_ids[:, None] == jnp.arange(lens.shape[0], dtype=jnp.int32)[None, :]
    begin = jnp.sum(jnp.where(chosen, starts[None, :], 0), axis=1)
    return (segment_ids, local - begin, starts)


def turn_heads(t, gain, cosine, sine):
    t = t * lax.rsqrt(jnp.mean(t * t, axis=-1, keepdims=True) + EPS) * gain
    return (t * cosine + pltpu.roll(t, HEAD_SIZE // 2, 1) * sine).astype(jnp.bfloat16)


def attend_kernel(chunk, kv_heads, q_heads, *refs):
    total, cosine, sine, begin, q_gain, k_gain = refs[:6]
    past_keys, past_values = refs[6 : 6 + chunk], refs[6 + chunk : 6 + 2 * chunk]
    attended, key_out, value_out = refs[6 + 2 * chunk :]
    rows = total.shape[0]
    group = q_heads // kv_heads
    kv_width = kv_heads * HEAD_SIZE
    cos, sin = cosine[...], sine[...]
    q_scale, k_scale = q_gain[...].astype(jnp.float32), k_gain[...].astype(jnp.float32)
    keys = (chunk + 1) * rows
    key_row = lax.broadcasted_iota(jnp.int32, (rows, keys), 1)
    query_row = lax.broadcasted_iota(jnp.int32, (rows, keys), 0) + chunk * rows
    allowed = (key_row <= query_row) & (key_row >= begin[...])
    value_out[...] = total[:, kv_width : 2 * kv_width].astype(jnp.bfloat16)
    for n in range(kv_heads):
        here = slice(n * HEAD_SIZE, (n + 1) * HEAD_SIZE)
        key_out[:, here] = turn_heads(total[:, here], k_scale, cos, sin)
        key = jnp.concatenate([k[:, here] for k in past_keys] + [key_out[:, here]], axis=0)
        value = jnp.concatenate([v[:, here] for v in past_values] + [value_out[:, here]], axis=0)
        for g in range(group):
            first = (n * group + g) * HEAD_SIZE
            query = turn_heads(
                total[:, 2 * kv_width + first : 2 * kv_width + first + HEAD_SIZE], q_scale, cos, sin
            )
            scores = lax.dot_general(
                query, key, (((1,), (1,)), ((), ())), preferred_element_type=jnp.float32
            ) / (HEAD_SIZE**0.5)
            scores = jnp.where(allowed, scores, -1e30)
            expo = jnp.exp(scores - jnp.max(scores, axis=-1, keepdims=True))
            weights = (expo / jnp.sum(expo, axis=-1, keepdims=True)).astype(jnp.bfloat16)
            attended[:, first : first + HEAD_SIZE] = jnp.dot(
                weights, value, preferred_element_type=jnp.float32
            ).astype(jnp.bfloat16)


def attend_chunk(chunk, total, cosine, sine, begin, q_gain, k_gain, keys, values, kv_width):
    rows = total.shape[0]
    q_width = total.shape[1] - 2 * kv_width
    flops = 4 * rows * (chunk + 1) * rows * q_width
    return pl.pallas_call(
        functools.partial(attend_kernel, chunk, kv_width // HEAD_SIZE, q_width // HEAD_SIZE),
        out_shape=(
            jax.ShapeDtypeStruct((rows, q_width), jnp.bfloat16),
            jax.ShapeDtypeStruct((rows, kv_width), jnp.bfloat16),
            jax.ShapeDtypeStruct((rows, kv_width), jnp.bfloat16),
        ),
        compiler_params=pltpu.CompilerParams(vmem_limit_bytes=32 * 2**20),
        cost_estimate=pl.CostEstimate(
            flops=4 * flops, bytes_accessed=4 * total.size, transcendentals=0
        ),
    )(total, cosine, sine, begin, q_gain, k_gain, *keys, *values)


def swap(block, axis, pairs):
    return lax.ppermute(block, axis, pairs)


def gather_kernel(n_groups, n_dp, cuts, *refs):
    local_sem, send_sem, recv_sem = refs[-3:]
    arrays = (len(refs) - 3) // 2
    shards, fulls = refs[:arrays], refs[arrays : 2 * arrays]
    chips = n_dp // 2
    me, group = lax.axis_index("dp"), lax.axis_index("groups")
    twin = me + 1 - 2 * lax.rem(me, 2)
    after, before = lax.rem(me + 2, n_dp), lax.rem(me - 2 + n_dp, n_dp)
    mesh_id = pl.DeviceIdType.MESH

    barrier = pltpu.get_barrier_semaphore()
    for peer in (twin, after, before):
        pl.semaphore_signal(barrier, inc=1, device_id={"dp": peer}, device_id_type=mesh_id)
    for turn in range(1, n_groups):
        peer = lax.rem(group + turn, n_groups)
        pl.semaphore_signal(barrier, inc=1, device_id={"groups": peer}, device_id_type=mesh_id)
    pl.semaphore_wait(barrier, 2 + n_groups)

    counter = [0]
    sent = []

    def slot():
        counter[0] += 1
        return counter[0] - 1

    def send(src, dst, index, target):
        copy = pltpu.make_async_remote_copy(
            src_ref=src,
            dst_ref=dst,
            send_sem=send_sem.at[index],
            recv_sem=recv_sem.at[index],
            device_id=target,
            device_id_type=mesh_id,
        )
        copy.start()
        sent.append(copy)

    def arrive(dst, index):
        pltpu.make_async_remote_copy(
            src_ref=dst,
            dst_ref=dst,
            send_sem=send_sem.at[index],
            recv_sem=recv_sem.at[index],
            device_id={"dp": twin},
            device_id_type=mesh_id,
        ).wait_recv()

    pending = []
    hops = {}
    for a in range(arrays):
        part = shards[a].shape[0] // (n_groups * cuts)
        for cut in range(cuts):
            rows = pl.ds((cut * n_groups + group) * part, part)
            hops[a, cut] = slot()
            send(shards[a].at[rows], fulls[a].at[me, rows], hops[a, cut], {"dp": after})
    for a in range(arrays):
        index = slot()
        send(shards[a], fulls[a].at[me], index, {"dp": twin})
        pending.append((fulls[a].at[twin], index))
    own = [pltpu.make_async_copy(shards[a], fulls[a].at[me], local_sem.at[a]) for a in range(arrays)]
    for copy in own:
        copy.start()
    for step in range(1, chips):
        owner = lax.rem(me - 2 * step + n_dp, n_dp)
        other = lax.rem(twin - 2 * step + n_dp, n_dp)
        trades = {}

        def from_groups(a, cut):
            part = shards[a].shape[0] // (n_groups * cuts)
            for turn in range(1, n_groups):
                source = lax.rem(group - turn + n_groups, n_groups)
                theirs = pl.ds((cut * n_groups + source) * part, part)
                arrive(fulls[a].at[owner, theirs], trades[a, cut, turn])
                index = slot()
                send(fulls[a].at[owner, theirs], fulls[a].at[owner, theirs], index, {"dp": twin})
                pending.append((fulls[a].at[other, theirs], index))

        work = [(a, cut) for a in range(arrays) for cut in range(cuts)]
        for place, (a, cut) in enumerate(work):
            part = shards[a].shape[0] // (n_groups * cuts)
            rows = pl.ds((cut * n_groups + group) * part, part)
            block = fulls[a].at[owner, rows]
            arrive(block, hops[a, cut])
            if step < chips - 1:
                hops[a, cut] = slot()
                send(block, block, hops[a, cut], {"dp": after})
            for turn in range(1, n_groups):
                trades[a, cut, turn] = slot()
                send(block, block, trades[a, cut, turn], {"groups": lax.rem(group + turn, n_groups)})
            index = slot()
            send(block, block, index, {"dp": twin})
            pending.append((fulls[a].at[other, rows], index))
            if place:
                from_groups(*work[place - 1])
        from_groups(*work[-1])
    for block, index in pending:
        arrive(block, index)
    for copy in own:
        copy.wait()
    for copy in sent:
        copy.wait_send()


def gather_shards(shards, n_groups, n_dp, cuts):
    chips = n_dp // 2
    copies = len(shards) * (1 + cuts * (chips - 1) * (1 + 2 * (n_groups - 1) + 1))
    return pl.pallas_call(
        functools.partial(gather_kernel, n_groups, n_dp, cuts),
        out_shape=[jax.ShapeDtypeStruct((n_dp,) + w.shape, w.dtype) for w in shards],
        in_specs=[pl.BlockSpec(memory_space=pl.ANY)] * len(shards),
        out_specs=[pl.BlockSpec(memory_space=pl.ANY)] * len(shards),
        scratch_shapes=[
            pltpu.SemaphoreType.DMA((len(shards),)),
            pltpu.SemaphoreType.DMA((copies,)),
            pltpu.SemaphoreType.DMA((copies,)),
        ],
        compiler_params=pltpu.CompilerParams(collective_id=0, has_side_effects=True),
        cost_estimate=pl.CostEstimate(flops=0, bytes_accessed=200 * 2**20, transcendentals=0),
    )(*shards)


def gather_rows(rows_block, n_dp):
    chips = n_dp // 2
    twin = [(i, i ^ 1) for i in range(n_dp)]
    onward = [(i, (i + 2) % n_dp) for i in range(n_dp)]
    me = lax.axis_index("dp")
    blocks = []
    piece = rows_block
    for step in range(chips):
        if step:
            piece = swap(piece, "dp", onward)
        owner = lax.rem(me - 2 * step + n_dp, n_dp)
        blocks.append((owner, piece))
        blocks.append((owner ^ 1, swap(piece, "dp", twin)))
    return blocks


def on_device(
    n_groups, n_dp, n_tensor, tokens, lengths, owner_slot, norm_gain, w_query, w_key, w_value, q_gain, k_gain, w_out
):
    token_rows = tokens.shape[0]
    rows_each = token_rows // CHUNKS
    kv_width = w_key.shape[1]
    depth = w_query.shape[0]
    wholes = [
        lax.all_gather(tokens[h * rows_each : (h + 1) * rows_each], "tensor", axis=1, tiled=True)
        for h in range(CHUNKS)
    ]
    w_all = jnp.concatenate([w_key, w_value, w_query], axis=1)
    in_parts, out_parts = gather_shards((w_all, w_out), n_groups, n_dp, 2)
    in_full = in_parts.reshape(n_dp * depth, w_all.shape[1])
    lens = lengths[0]
    segment_ids, positions, starts = layout(lens, token_rows)
    begin = (jnp.arange(token_rows, dtype=jnp.int32) - positions)[:, None]
    freq = THETA ** (-(2.0 * jnp.arange(HEAD_SIZE // 2, dtype=jnp.float32)) / HEAD_SIZE)
    angle = positions.astype(jnp.float32)[:, None] * freq[None, :]
    cosine, sine = jnp.cos(angle), jnp.sin(angle)
    cosine = jnp.concatenate([cosine, cosine], axis=1)
    sine = jnp.concatenate([-sine, sine], axis=1)

    keys, values, mixed = [], [], []
    last = None
    for h in range(CHUNKS):
        here = slice(h * rows_each, (h + 1) * rows_each)
        whole = wholes[h]
        if last is not None:
            whole, last = lax.optimization_barrier((whole, last))
        if h == CHUNKS - 1:
            whole, mixed[0] = lax.optimization_barrier((whole, mixed[0]))
        wide = whole.astype(jnp.float32)
        normed = (
            wide
            * lax.rsqrt(jnp.mean(wide * wide, axis=-1, keepdims=True) + EPS)
            * norm_gain.astype(jnp.float32)
        ).astype(jnp.bfloat16)
        total = jnp.dot(normed, in_full, preferred_element_type=jnp.float32)
        attended_rows, key, value = attend_chunk(
            h, total, cosine[here], sine[here], begin[here], q_gain[None], k_gain[None], keys, values, kv_width
        )
        keys.append(key)
        values.append(value)
        term = jnp.concatenate(
            [
                jnp.dot(attended_rows, out_parts[d], preferred_element_type=jnp.float32).astype(
                    jnp.bfloat16
                )
                for d in range(n_dp)
            ],
            axis=1,
        )
        last = term
        width = tokens.shape[1]
        rank = lax.axis_index("tensor")
        if h == 0:
            summed = lax.dynamic_slice_in_dim(term, rank * width, width, 1).astype(jnp.float32)
            for turn in range(1, n_tensor):
                target = lax.rem(rank + turn, n_tensor)
                piece = lax.dynamic_slice_in_dim(term, target * width, width, 1)
                got = swap(piece, "tensor", [(i, (i + turn) % n_tensor) for i in range(n_tensor)])
                summed = summed + got.astype(jnp.float32)
        else:
            summed = lax.psum_scatter(term, "tensor", scatter_dimension=1, tiled=True).astype(
                jnp.float32
            )
        mixed.append((tokens[here].astype(jnp.float32) + summed).astype(jnp.bfloat16))

    pair = jnp.concatenate(
        [
            jnp.concatenate(keys, axis=0),
            jnp.concatenate(values, axis=0),
        ],
        axis=1,
    )
    stack = jnp.zeros((n_dp * token_rows + MOST, 2 * kv_width), jnp.bfloat16)
    for owner, block in gather_rows(pair, n_dp):
        stack = lax.dynamic_update_slice(stack, block, (owner * token_rows, 0))
    every_length = jnp.zeros((n_dp, PROMPTS), jnp.int32)
    for owner, block in gather_rows(lengths, n_dp):
        every_length = lax.dynamic_update_slice(every_length, block, (owner, 0))
    replica = lax.axis_index("dp")
    slots = []
    for p in range(PROMPTS):
        prompt = jnp.argmax(owner_slot == replica * PROMPTS + p).astype(jnp.int32)
        length = every_length[prompt // PROMPTS, prompt % PROMPTS]
        before = jnp.where(
            jnp.arange(PROMPTS) < prompt % PROMPTS, every_length[prompt // PROMPTS], 0
        ).sum()
        block = lax.dynamic_slice_in_dim(
            stack, prompt // PROMPTS * token_rows + before, MOST, 0
        )
        live = jnp.arange(MOST, dtype=jnp.int32)[:, None] < length
        slots.append(jnp.where(live, block, jnp.zeros_like(block)))
    cache = jnp.stack(slots, axis=0)
    return (jnp.concatenate(mixed, axis=0), cache[..., :kv_width], cache[..., kv_width:])


def solution(mesh):
    return jax.shard_map(
        functools.partial(on_device, mesh.shape["groups"], mesh.shape["dp"], mesh.shape["tensor"]),
        mesh=mesh,
        in_specs=(
            P(("groups", "dp"), "tensor"),
            P(("groups", "dp"), None),
            P("groups"),
            P(),
            P("dp", "tensor"),
            P("dp", "tensor"),
            P("dp", "tensor"),
            P(),
            P(),
            P("tensor", "dp"),
        ),
        out_specs=(
            P(("groups", "dp"), "tensor"),
            P(("groups", "dp"), None, "tensor"),
            P(("groups", "dp"), None, "tensor"),
        ),
        check_vma=False,
    )
```

```python
import functools

import jax
import jax.numpy as jnp
from jax import lax
from jax.experimental import pallas as pl
from jax.experimental.pallas import tpu as pltpu
from jax.sharding import PartitionSpec as P

HEAD_SIZE = 128
PROMPTS = 2
MOST = 576
CHUNKS = 3
AHEAD = 2


EPS = 1e-06
THETA = 1000000.0


def layout(lens, token_rows):
    local = jnp.arange(token_rows, dtype=jnp.int32)
    ends = jnp.cumsum(lens)
    starts = ends - lens
    segment_ids = jnp.sum((local[:, None] >= ends[None, :]).astype(jnp.int32), axis=1)
    chosen = segment_ids[:, None] == jnp.arange(lens.shape[0], dtype=jnp.int32)[None, :]
    begin = jnp.sum(jnp.where(chosen, starts[None, :], 0), axis=1)
    return (segment_ids, local - begin, starts)


def turn_heads(t, gain, cosine, sine):
    t = t * lax.rsqrt(jnp.mean(t * t, axis=-1, keepdims=True) + EPS) * gain
    return (t * cosine + pltpu.roll(t, HEAD_SIZE // 2, 1) * sine).astype(jnp.bfloat16)


def attend_kernel(chunk, kv_heads, q_heads, *refs):
    total, cosine, sine, begin, q_gain, k_gain = refs[:6]
    past_keys, past_values = refs[6 : 6 + chunk], refs[6 + chunk : 6 + 2 * chunk]
    attended, key_out, value_out = refs[6 + 2 * chunk :]
    rows = total.shape[0]
    group = q_heads // kv_heads
    kv_width = kv_heads * HEAD_SIZE
    cos, sin = cosine[...], sine[...]
    q_scale, k_scale = q_gain[...].astype(jnp.float32), k_gain[...].astype(jnp.float32)
    keys = (chunk + 1) * rows
    key_row = lax.broadcasted_iota(jnp.int32, (rows, keys), 1)
    query_row = lax.broadcasted_iota(jnp.int32, (rows, keys), 0) + chunk * rows
    allowed = (key_row <= query_row) & (key_row >= begin[...])
    value_out[...] = total[:, kv_width : 2 * kv_width].astype(jnp.bfloat16)
    for n in range(kv_heads):
        here = slice(n * HEAD_SIZE, (n + 1) * HEAD_SIZE)
        key_out[:, here] = turn_heads(total[:, here], k_scale, cos, sin)
        key = jnp.concatenate([k[:, here] for k in past_keys] + [key_out[:, here]], axis=0)
        value = jnp.concatenate([v[:, here] for v in past_values] + [value_out[:, here]], axis=0)
        for g in range(group):
            first = (n * group + g) * HEAD_SIZE
            query = turn_heads(
                total[:, 2 * kv_width + first : 2 * kv_width + first + HEAD_SIZE], q_scale, cos, sin
            )
            scores = lax.dot_general(
                query, key, (((1,), (1,)), ((), ())), preferred_element_type=jnp.float32
            ) / (HEAD_SIZE**0.5)
            scores = jnp.where(allowed, scores, -1e30)
            expo = jnp.exp(scores - jnp.max(scores, axis=-1, keepdims=True))
            weights = (expo / jnp.sum(expo, axis=-1, keepdims=True)).astype(jnp.bfloat16)
            attended[:, first : first + HEAD_SIZE] = jnp.dot(
                weights, value, preferred_element_type=jnp.float32
            ).astype(jnp.bfloat16)


def attend_chunk(chunk, total, cosine, sine, begin, q_gain, k_gain, keys, values, kv_width):
    rows = total.shape[0]
    q_width = total.shape[1] - 2 * kv_width
    flops = 4 * rows * (chunk + 1) * rows * q_width
    return pl.pallas_call(
        functools.partial(attend_kernel, chunk, kv_width // HEAD_SIZE, q_width // HEAD_SIZE),
        out_shape=(
            jax.ShapeDtypeStruct((rows, q_width), jnp.bfloat16),
            jax.ShapeDtypeStruct((rows, kv_width), jnp.bfloat16),
            jax.ShapeDtypeStruct((rows, kv_width), jnp.bfloat16),
        ),
        compiler_params=pltpu.CompilerParams(vmem_limit_bytes=32 * 2**20),
        cost_estimate=pl.CostEstimate(
            flops=4 * flops, bytes_accessed=4 * total.size, transcendentals=0
        ),
    )(total, cosine, sine, begin, q_gain, k_gain, *keys, *values)


def swap(block, axis, pairs):
    return lax.ppermute(block, axis, pairs)


def gather_kernel(n_groups, n_dp, cuts, *refs):
    send_sem, recv_sem = refs[-2:]
    arrays = (len(refs) - 2) // 2
    shards, fulls = refs[:arrays], refs[arrays : 2 * arrays]
    chips = n_dp // 2
    me, group = lax.axis_index("dp"), lax.axis_index("groups")
    twin = me + 1 - 2 * lax.rem(me, 2)
    after, before = lax.rem(me + 2, n_dp), lax.rem(me - 2 + n_dp, n_dp)
    mesh_id = pl.DeviceIdType.MESH

    barrier = pltpu.get_barrier_semaphore()
    for peer in (twin, after, before):
        pl.semaphore_signal(barrier, inc=1, device_id={"dp": peer}, device_id_type=mesh_id)
    for turn in range(1, n_groups):
        peer = lax.rem(group + turn, n_groups)
        pl.semaphore_signal(barrier, inc=1, device_id={"groups": peer}, device_id_type=mesh_id)
    pl.semaphore_wait(barrier, 2 + n_groups)

    counter = [0]
    sent = []

    def slot():
        counter[0] += 1
        return counter[0] - 1

    def send(src, dst, index, target):
        copy = pltpu.make_async_remote_copy(
            src_ref=src,
            dst_ref=dst,
            send_sem=send_sem.at[index],
            recv_sem=recv_sem.at[index],
            device_id=target,
            device_id_type=mesh_id,
        )
        copy.start()
        sent.append(copy)

    def arrive(dst, index):
        pltpu.make_async_remote_copy(
            src_ref=dst,
            dst_ref=dst,
            send_sem=send_sem.at[index],
            recv_sem=recv_sem.at[index],
            device_id={"dp": twin},
            device_id_type=mesh_id,
        ).wait_recv()

    pending = []
    hops = {}
    work = [(a, cut) for a in range(arrays) for cut in range(cuts)]

    def first_hop(a, cut):
        part = shards[a].shape[0] // (n_groups * cuts)
        rows = pl.ds((cut * n_groups + group) * part, part)
        hops[a, cut] = slot()
        send(shards[a].at[rows], fulls[a].at[me, rows], hops[a, cut], {"dp": after})

    for a, cut in work[:AHEAD]:
        first_hop(a, cut)
    for a in range(arrays):
        index = slot()
        send(shards[a], fulls[a].at[me], index, {"dp": twin})
        pending.append((fulls[a].at[twin], index))
    for step in range(1, chips):
        owner = lax.rem(me - 2 * step + n_dp, n_dp)
        other = lax.rem(twin - 2 * step + n_dp, n_dp)
        trades = {}

        def from_groups(a, cut):
            part = shards[a].shape[0] // (n_groups * cuts)
            for turn in range(1, n_groups):
                source = lax.rem(group - turn + n_groups, n_groups)
                theirs = pl.ds((cut * n_groups + source) * part, part)
                arrive(fulls[a].at[owner, theirs], trades[a, cut, turn])
                index = slot()
                send(fulls[a].at[owner, theirs], fulls[a].at[owner, theirs], index, {"dp": twin})
                pending.append((fulls[a].at[other, theirs], index))

        for place, (a, cut) in enumerate(work):
            part = shards[a].shape[0] // (n_groups * cuts)
            rows = pl.ds((cut * n_groups + group) * part, part)
            block = fulls[a].at[owner, rows]
            arrive(block, hops[a, cut])
            if step == 1 and place + AHEAD < len(work):
                first_hop(*work[place + AHEAD])
            if step < chips - 1:
                hops[a, cut] = slot()
                send(block, block, hops[a, cut], {"dp": after})
            for turn in range(1, n_groups):
                trades[a, cut, turn] = slot()
                send(block, block, trades[a, cut, turn], {"groups": lax.rem(group + turn, n_groups)})
            index = slot()
            send(block, block, index, {"dp": twin})
            pending.append((fulls[a].at[other, rows], index))
            if place:
                from_groups(*work[place - 1])
        from_groups(*work[-1])
    for block, index in pending:
        arrive(block, index)
    for copy in sent:
        copy.wait_send()


def gather_shards(shards, n_groups, n_dp, cuts):
    chips = n_dp // 2
    copies = len(shards) * (1 + cuts * (chips - 1) * (1 + 2 * (n_groups - 1) + 1))
    fulls = pl.pallas_call(
        functools.partial(gather_kernel, n_groups, n_dp, cuts),
        out_shape=[jax.ShapeDtypeStruct((n_dp,) + w.shape, w.dtype) for w in shards],
        in_specs=[pl.BlockSpec(memory_space=pl.ANY)] * len(shards),
        out_specs=[pl.BlockSpec(memory_space=pl.ANY)] * len(shards),
        scratch_shapes=[
            pltpu.SemaphoreType.DMA((copies,)),
            pltpu.SemaphoreType.DMA((copies,)),
        ],
        compiler_params=pltpu.CompilerParams(collective_id=0, has_side_effects=True),
        cost_estimate=pl.CostEstimate(flops=0, bytes_accessed=200 * 2**20, transcendentals=0),
    )(*shards)
    me = lax.axis_index("dp")
    return [
        lax.dynamic_update_slice(full, shard[None], (me, 0, 0)) for full, shard in zip(fulls, shards)
    ]


def gather_rows(rows_block, n_dp):
    chips = n_dp // 2
    twin = [(i, i ^ 1) for i in range(n_dp)]
    onward = [(i, (i + 2) % n_dp) for i in range(n_dp)]
    me = lax.axis_index("dp")
    blocks = []
    piece = rows_block
    for step in range(chips):
        if step:
            piece = swap(piece, "dp", onward)
        owner = lax.rem(me - 2 * step + n_dp, n_dp)
        blocks.append((owner, piece))
        blocks.append((owner ^ 1, swap(piece, "dp", twin)))
    return blocks


def on_device(
    n_groups, n_dp, n_tensor, tokens, lengths, owner_slot, norm_gain, w_query, w_key, w_value, q_gain, k_gain, w_out
):
    token_rows = tokens.shape[0]
    rows_each = token_rows // CHUNKS
    kv_width = w_key.shape[1]
    depth = w_query.shape[0]
    wholes = [
        lax.all_gather(tokens[h * rows_each : (h + 1) * rows_each], "tensor", axis=1, tiled=True)
        for h in range(CHUNKS)
    ]
    w_all = jnp.concatenate([w_key, w_value, w_query], axis=1)
    in_parts, out_parts = gather_shards((w_all, w_out), n_groups, n_dp, 2)
    in_full = in_parts.reshape(n_dp * depth, w_all.shape[1])
    lens = lengths[0]
    segment_ids, positions, starts = layout(lens, token_rows)
    begin = (jnp.arange(token_rows, dtype=jnp.int32) - positions)[:, None]
    freq = THETA ** (-(2.0 * jnp.arange(HEAD_SIZE // 2, dtype=jnp.float32)) / HEAD_SIZE)
    angle = positions.astype(jnp.float32)[:, None] * freq[None, :]
    cosine, sine = jnp.cos(angle), jnp.sin(angle)
    cosine = jnp.concatenate([cosine, cosine], axis=1)
    sine = jnp.concatenate([-sine, sine], axis=1)

    keys, values, mixed = [], [], []
    last = None
    for h in range(CHUNKS):
        here = slice(h * rows_each, (h + 1) * rows_each)
        whole = wholes[h]
        if last is not None:
            whole, last = lax.optimization_barrier((whole, last))
        if h == CHUNKS - 1:
            whole, mixed[0] = lax.optimization_barrier((whole, mixed[0]))
        wide = whole.astype(jnp.float32)
        normed = (
            wide
            * lax.rsqrt(jnp.mean(wide * wide, axis=-1, keepdims=True) + EPS)
            * norm_gain.astype(jnp.float32)
        ).astype(jnp.bfloat16)
        total = jnp.dot(normed, in_full, preferred_element_type=jnp.float32)
        attended_rows, key, value = attend_chunk(
            h, total, cosine[here], sine[here], begin[here], q_gain[None], k_gain[None], keys, values, kv_width
        )
        keys.append(key)
        values.append(value)
        term = jnp.concatenate(
            [
                jnp.dot(attended_rows, out_parts[d], preferred_element_type=jnp.float32).astype(
                    jnp.bfloat16
                )
                for d in range(n_dp)
            ],
            axis=1,
        )
        last = term
        width = tokens.shape[1]
        rank = lax.axis_index("tensor")
        if h == 0:
            summed = lax.dynamic_slice_in_dim(term, rank * width, width, 1).astype(jnp.float32)
            for turn in range(1, n_tensor):
                target = lax.rem(rank + turn, n_tensor)
                piece = lax.dynamic_slice_in_dim(term, target * width, width, 1)
                got = swap(piece, "tensor", [(i, (i + turn) % n_tensor) for i in range(n_tensor)])
                summed = summed + got.astype(jnp.float32)
        else:
            summed = lax.psum_scatter(term, "tensor", scatter_dimension=1, tiled=True).astype(
                jnp.float32
            )
        mixed.append((tokens[here].astype(jnp.float32) + summed).astype(jnp.bfloat16))

    pair = jnp.concatenate(
        [
            jnp.concatenate(keys, axis=0),
            jnp.concatenate(values, axis=0),
        ],
        axis=1,
    )
    stack = jnp.zeros((n_dp * token_rows + MOST, 2 * kv_width), jnp.bfloat16)
    for owner, block in gather_rows(pair, n_dp):
        stack = lax.dynamic_update_slice(stack, block, (owner * token_rows, 0))
    every_length = jnp.zeros((n_dp, PROMPTS), jnp.int32)
    for owner, block in gather_rows(lengths, n_dp):
        every_length = lax.dynamic_update_slice(every_length, block, (owner, 0))
    replica = lax.axis_index("dp")
    slots = []
    for p in range(PROMPTS):
        prompt = jnp.argmax(owner_slot == replica * PROMPTS + p).astype(jnp.int32)
        length = every_length[prompt // PROMPTS, prompt % PROMPTS]
        before = jnp.where(
            jnp.arange(PROMPTS) < prompt % PROMPTS, every_length[prompt // PROMPTS], 0
        ).sum()
        block = lax.dynamic_slice_in_dim(
            stack, prompt // PROMPTS * token_rows + before, MOST, 0
        )
        live = jnp.arange(MOST, dtype=jnp.int32)[:, None] < length
        slots.append(jnp.where(live, block, jnp.zeros_like(block)))
    cache = jnp.stack(slots, axis=0)
    return (jnp.concatenate(mixed, axis=0), cache[..., :kv_width], cache[..., kv_width:])


def solution(mesh):
    return jax.shard_map(
        functools.partial(on_device, mesh.shape["groups"], mesh.shape["dp"], mesh.shape["tensor"]),
        mesh=mesh,
        in_specs=(
            P(("groups", "dp"), "tensor"),
            P(("groups", "dp"), None),
            P("groups"),
            P(),
            P("dp", "tensor"),
            P("dp", "tensor"),
            P("dp", "tensor"),
            P(),
            P(),
            P("tensor", "dp"),
        ),
        out_specs=(
            P(("groups", "dp"), "tensor"),
            P(("groups", "dp"), None, "tensor"),
            P(("groups", "dp"), None, "tensor"),
        ),
        check_vma=False,
    )
```
